32 devices in a mesh: chan: 8 (over z, y), tm: 4 (over x, core).
Axes of the slice: x: 2, y: 2, z: 4, core: 2. Of those that a mesh axis runs over, the one named last changes fastest.
Arguments:
- voltages: bfloat16 [32, 128, 2, 1024], P('chan', 'tm'), may hold values from -6 to 6
- filter_taps: float32 [12, 1024], replicated, may hold values from -1.75 to 1.75
- flagged: int32 [256], replicated, may hold values from 0 to 1023, as said below
- owners: int32 [1024], replicated, may hold values from 0 to 31, as said below
Outputs:
- visibilities: float32 [1024, 2, 32, 32], P(('chan', 'tm'))
The draws below stay inside these ranges and needn't reach their ends.
Inputs may be any that keep to these rules, and one draw needn't show every extreme that they name: `flagged`: distinct channel numbers. `owners`: each device owns exactly 32 of the 1024 channels, flagged or not; device d is the one with chan index d // 4 and tm index d % 4.
All inputs are finite; a program needn't handle non-finite values.
Results may differ from the reference program's by a relative error of at most 0.0059.
Values may be sent and summed in bfloat16 or wider, within the bound.
A program may use at most 64 MiB of HBM per device.

```python
import math
import jax
import jax.numpy as jnp
from jax import lax

INPUTS = 32
NCHAN = 1024
TAPS = 12
SPECTRA = 128
NFLAG = 256
CAP = 32


def draw_flagged(key, part):
    shuffled = jax.random.permutation(jax.random.fold_in(key, 11), NCHAN)
    return shuffled[:NFLAG].astype(jnp.int32)


def draw_owners(key, part):
    shuffled = jax.random.permutation(jax.random.fold_in(key, 23), NCHAN).astype(jnp.int32)
    inverse = jnp.argsort(shuffled, stable=True).astype(jnp.int32)
    return (inverse // CAP).astype(jnp.int32)


def shard_levels(stream_key, shape, split, low, high):
    level = 1.0
    for position, shards_of in split:
        heights = jax.random.uniform(jax.random.fold_in(jax.random.fold_in(stream_key, 6), position), (shards_of,), jnp.float32, low / len(split), high / len(split))
        level = level * jnp.repeat(jnp.exp(heights), shape[position] // shards_of).reshape((-1,) + (1,) * (len(shape) - 1 - position))
    return level


def bell_draw(stream_key, dims, width, bound, split=(), held_as=jnp.bfloat16):
    array = width * jax.random.normal(stream_key, dims, jnp.float32)
    if split:
        array = array * shard_levels(stream_key, dims, split, -0.22, 0.18)
    return jnp.clip(array, -bound, bound).astype(held_as)


def setup_inputs(seed: int = 0) -> dict:
    arg_keys = jax.random.split(jax.random.key(seed), 5)
    return {
        "voltages": bell_draw(arg_keys[0], (INPUTS, SPECTRA, 2, NCHAN), 1.0, 6.0, ((0, 8), (1, 4))),
        "filter_taps": bell_draw(arg_keys[1], (TAPS, NCHAN), TAPS ** -0.5, 1.75, (), jnp.float32),
        "flagged": draw_flagged(jax.random.fold_in(arg_keys[4], 71), 0),
        "owners": draw_owners(jax.random.fold_in(arg_keys[4], 71), 0),
    }


def dft_tables(channels):
    positions = jnp.arange(channels, dtype=jnp.int32)
    phases = positions[:, None] * positions[None, :] % channels
    angles = phases.astype(jnp.float32) * (2.0 * math.pi / channels)
    factor = 1.0 / math.sqrt(channels)
    return ((jnp.cos(angles) * factor).astype(jnp.bfloat16), (jnp.sin(angles) * factor).astype(jnp.bfloat16))

def slot_table(flagged, owners, channels, capacity):
    channel_ids = jnp.arange(channels, dtype=jnp.int32)
    alive_mask = jnp.logical_not(jnp.any(flagged[:, None] == channel_ids[None, :], axis=0))
    earlier = (owners[None, :] == owners[:, None]) & alive_mask[None, :] & (channel_ids[None, :] < channel_ids[:, None])
    order_rank = lax.optimization_barrier(jnp.sum(earlier.astype(jnp.int32), axis=1))
    slot_of = owners * capacity + order_rank
    matches = (slot_of[None, :] == channel_ids[:, None]) & alive_mask[None, :]
    present = jnp.any(matches, axis=1)
    chosen = lax.optimization_barrier(jnp.sum(jnp.where(matches, channel_ids[None, :], 0), axis=1)).astype(jnp.int32)
    return (chosen, present)

def channelize(samples, filter_taps, cos_table, sin_table):
    widened = samples.astype(jnp.float32)
    padded = jnp.pad(widened, ((TAPS - 1, 0), (0, 0), (0, 0)))
    running = jnp.zeros(widened.shape, jnp.float32)
    for tap_index in range(TAPS):
        start_row = TAPS - 1 - tap_index
        running = running + filter_taps[tap_index][None, None, :] * padded[start_row:start_row + SPECTRA]
    filtered = running.astype(jnp.bfloat16)
    flat_rows = filtered.reshape(SPECTRA * 2, NCHAN)
    cos_part = jnp.dot(flat_rows, cos_table, preferred_element_type=jnp.float32).reshape(SPECTRA, 2, NCHAN)
    sin_part = jnp.dot(flat_rows, sin_table, preferred_element_type=jnp.float32).reshape(SPECTRA, 2, NCHAN)
    real_part = cos_part[:, 0] + sin_part[:, 1]
    imag_part = cos_part[:, 1] - sin_part[:, 0]
    return jnp.stack([real_part, imag_part], axis=1).astype(jnp.bfloat16)

def correlate(slot_block):
    real_part = slot_block[0]
    imag_part = slot_block[1]
    first_rows = jnp.concatenate([real_part, imag_part], axis=1)
    second_rows = jnp.concatenate([imag_part, -real_part], axis=1)
    vis_real = jnp.dot(first_rows, first_rows.T, preferred_element_type=jnp.float32)
    vis_imag = jnp.dot(second_rows, first_rows.T, preferred_element_type=jnp.float32)
    return jnp.stack([vis_real, vis_imag], axis=0) / SPECTRA

def reference(voltages, filter_taps, flagged, owners):
    cos_table, sin_table = dft_tables(NCHAN)

    def one_input(samples):
        return channelize(samples, filter_taps, cos_table, sin_table)
    spectra = lax.map(one_input, voltages)
    chosen, present = slot_table(flagged, owners, NCHAN, CAP)
    picked = jnp.take(spectra, chosen, axis=3)
    picked = jnp.where(present[None, None, None, :], picked, jnp.zeros((), jnp.bfloat16))
    per_slot = jnp.transpose(picked, (3, 2, 0, 1))
    return lax.map(correlate, per_slot)
```

```python
import math

import jax
import jax.numpy as jnp
import numpy as np
from jax import lax
from jax.sharding import PartitionSpec as P


def dft_table(channels):
    positions = np.arange(channels, dtype=np.int32)
    phases = positions[:, None] * positions[None, :] % channels
    angles = phases.astype(np.float32) * np.float32(2.0 * math.pi / channels)
    factor = np.float32(1.0 / math.sqrt(channels))
    table = np.concatenate([np.cos(angles) * factor, np.sin(angles) * factor], axis=1)
    return jnp.asarray(table.astype(jnp.bfloat16))


def slot_matrix(flagged, owners, channels, capacity):
    ids = jnp.arange(channels, dtype=jnp.int32)
    alive = jnp.logical_not(jnp.any(flagged[:, None] == ids[None, :], axis=0))
    earlier = (owners[None, :] == owners[:, None]) & alive[None, :] & (ids[None, :] < ids[:, None])
    rank = jnp.sum(earlier.astype(jnp.int32), axis=1)
    slot_of = jnp.where(alive, owners * capacity + rank, -1)
    return (slot_of[None, :] == ids[:, None]).astype(jnp.bfloat16)


def local(voltages, filter_taps, flagged, owners):
    inp_dev, spec_dev, _, channels = voltages.shape
    taps = filter_taps.shape[0]
    devices = lax.axis_size("chan") * lax.axis_size("tm")
    capacity = channels // devices
    picks = slot_matrix(flagged, owners, channels, capacity)
    mine = lax.all_to_all(voltages, "tm", split_axis=0, concat_axis=1, tiled=True)
    stations, spectra_all = mine.shape[:2]
    samples = mine.transpose(0, 2, 1, 3).astype(jnp.float32)
    padded = jnp.pad(samples, ((0, 0), (0, 0), (taps - 1, 0), (0, 0)))
    running = jnp.zeros(samples.shape, jnp.float32)
    for tap in range(taps):
        start = taps - 1 - tap
        running = running + filter_taps[tap] * padded[:, :, start : start + spectra_all]
    filtered = running.astype(jnp.bfloat16)
    turned = jnp.stack([filtered[:, 1], -filtered[:, 0]], axis=1)
    rows = stations * 2 * spectra_all
    both = jnp.concatenate([filtered, turned], axis=-1).reshape(rows, 2 * channels)
    spectra = lax.dot_general(
        dft_table(channels), both, (((1,), (1,)), ((), ())), preferred_element_type=jnp.float32
    ).astype(jnp.bfloat16)
    chosen = jnp.dot(picks, spectra, preferred_element_type=jnp.float32).astype(jnp.bfloat16)
    sending = chosen.reshape(devices, capacity, rows)
    received = lax.all_to_all(sending, ("chan", "tm"), split_axis=0, concat_axis=0, tiled=True)
    parts = received.reshape(devices, capacity, stations, 2 * spectra_all).transpose(1, 0, 2, 3)
    first = parts.reshape(capacity, devices * stations, 2 * spectra_all)
    second = jnp.concatenate([first[..., spectra_all:], -first[..., :spectra_all]], axis=-1)
    stacked = jnp.stack([first, second], axis=1)
    total = jnp.einsum("cpit,cjt->cpij", stacked, first, preferred_element_type=jnp.float32)
    return total / spectra_all


def solution(mesh):
    return jax.shard_map(
        local,
        mesh=mesh,
        in_specs=(P("chan", "tm", None, None), P(), P(), P()),
        out_specs=P(("chan", "tm"), None, None, None),
        check_vma=False,
    )
```

```python
import functools
import math

import jax
import jax.numpy as jnp
import numpy as np
from jax import lax
from jax.experimental import pallas as pl
from jax.experimental.pallas import tpu as pltpu
from jax.sharding import PartitionSpec as P


def dft_table(channels):
    positions = np.arange(channels, dtype=np.int32)
    phases = positions[:, None] * positions[None, :] % channels
    angles = phases.astype(np.float32) * np.float32(2.0 * math.pi / channels)
    factor = np.float32(1.0 / math.sqrt(channels))
    table = np.concatenate([np.cos(angles) * factor, np.sin(angles) * factor], axis=1)
    return jnp.asarray(table.astype(jnp.bfloat16))


def slot_matrix(flagged, owners, channels, capacity):
    ids = jnp.arange(channels, dtype=jnp.int32)
    alive = jnp.logical_not(jnp.any(flagged[:, None] == ids[None, :], axis=0))
    earlier = (owners[None, :] == owners[:, None]) & alive[None, :] & (ids[None, :] < ids[:, None])
    rank = jnp.sum(earlier.astype(jnp.int32), axis=1)
    slot_of = jnp.where(alive, owners * capacity + rank, -1)
    return (slot_of[None, :] == ids[:, None]).astype(jnp.bfloat16)


GROUP_ROWS = 256
MESH = pl.DeviceIdType.MESH


def turn_kernel(chans, times, both_ref, table, picks_ref, got_ref, spectra, sending, send_sem, recv_sem):
    devices = chans * times
    capacity = sending.shape[1]
    channels = table.shape[0]
    per_group = GROUP_ROWS // capacity
    groups = devices // per_group
    me = lax.axis_index("chan") * times + lax.axis_index("tm")

    barrier = pltpu.get_barrier_semaphore()

    def greet(step, carry):
        other = lax.rem(me + step, devices)
        pl.semaphore_signal(barrier, inc=1, device_id=(other // times, lax.rem(other, times)), device_id_type=MESH)
        return carry

    lax.fori_loop(1, devices, greet, 0)

    def block_copy(slot_block, source, other):
        return pltpu.make_async_remote_copy(
            src_ref=sending.at[slot_block],
            dst_ref=got_ref.at[source],
            send_sem=send_sem.at[slot_block],
            recv_sem=recv_sem.at[source],
            device_id=(other // times, lax.rem(other, times)),
            device_id_type=MESH,
        )

    def transform(step, carry):
        rows = pl.ds(pl.multiple_of(step * GROUP_ROWS, GROUP_ROWS), GROUP_ROWS)
        spectra[rows, :] = lax.dot_general(
            table[rows, :], both_ref[...], (((1,), (1,)), ((), ())), preferred_element_type=jnp.float32
        ).astype(jnp.bfloat16)
        return carry

    lax.fori_loop(0, channels // GROUP_ROWS, transform, 0)
    pl.semaphore_wait(barrier, devices - 1)

    def send_group(step, carry):
        group = lax.rem(me // per_group + groups // 2 + step, groups)
        rows = pl.ds(pl.multiple_of(group * GROUP_ROWS, GROUP_ROWS), GROUP_ROWS)
        chosen = jnp.dot(picks_ref[rows, :], spectra[...], preferred_element_type=jnp.float32)
        sending[pl.ds(group * per_group, per_group)] = chosen.astype(jnp.bfloat16).reshape(
            per_group, capacity, chosen.shape[1]
        )

        def send(position, inner):
            other = group * per_group + lax.rem(me + position, per_group)

            @pl.when(other != me)
            def _():
                block_copy(other, me, other).start()

            return inner

        lax.fori_loop(0, per_group, send, 0)
        return carry

    lax.fori_loop(0, groups, send_group, 0)
    got_ref[me] = sending[me]

    def finish(step, carry):
        other = lax.rem(me + step, devices)
        copy = block_copy(other, other, other)
        copy.wait_send()
        copy.wait_recv()
        return carry

    lax.fori_loop(1, devices, finish, 0)


def turn(both, table, picks, chans, times, capacity):
    devices = chans * times
    rows = both.shape[0]
    channels = table.shape[0]
    return pl.pallas_call(
        functools.partial(turn_kernel, chans, times),
        out_shape=jax.ShapeDtypeStruct((devices, capacity, rows), jnp.bfloat16),
        in_specs=[pl.BlockSpec(memory_space=pltpu.VMEM)] * 3,
        out_specs=pl.BlockSpec(memory_space=pltpu.VMEM),
        scratch_shapes=[
            pltpu.VMEM((channels, rows), jnp.bfloat16),
            pltpu.VMEM((devices, capacity, rows), jnp.bfloat16),
            pltpu.SemaphoreType.DMA((devices,)),
            pltpu.SemaphoreType.DMA((devices,)),
        ],
        compiler_params=pltpu.CompilerParams(
            collective_id=0, has_side_effects=True, vmem_limit_bytes=32 * 1024 * 1024
        ),
    )(both, table, picks)


def local(voltages, filter_taps, flagged, owners):
    inp_dev, spec_dev, _, channels = voltages.shape
    taps = filter_taps.shape[0]
    devices = lax.axis_size("chan") * lax.axis_size("tm")
    capacity = channels // devices
    picks = slot_matrix(flagged, owners, channels, capacity)
    mine = lax.all_to_all(voltages, "tm", split_axis=0, concat_axis=1, tiled=True)
    stations, spectra_all = mine.shape[:2]
    samples = mine.transpose(0, 2, 1, 3).astype(jnp.float32)
    padded = jnp.pad(samples, ((0, 0), (0, 0), (taps - 1, 0), (0, 0)))
    running = jnp.zeros(samples.shape, jnp.float32)
    for tap in range(taps):
        start = taps - 1 - tap
        running = running + filter_taps[tap] * padded[:, :, start : start + spectra_all]
    filtered = running.astype(jnp.bfloat16)
    turned = jnp.stack([filtered[:, 1], -filtered[:, 0]], axis=1)
    rows = stations * 2 * spectra_all
    both = jnp.concatenate([filtered, turned], axis=-1).reshape(rows, 2 * channels)
    table = dft_table(channels)
    if capacity % 16 == 0 and GROUP_ROWS % capacity == 0 and channels % GROUP_ROWS == 0:
        received = turn(both, table, picks, lax.axis_size("chan"), lax.axis_size("tm"), capacity)
    else:
        spectra = lax.dot_general(
            table, both, (((1,), (1,)), ((), ())), preferred_element_type=jnp.float32
        ).astype(jnp.bfloat16)
        chosen = jnp.dot(picks, spectra, preferred_element_type=jnp.float32).astype(jnp.bfloat16)
        sending = chosen.reshape(devices, capacity, rows)
        received = lax.all_to_all(sending, ("chan", "tm"), split_axis=0, concat_axis=0, tiled=True)
    parts = received.reshape(devices, capacity, stations, 2 * spectra_all).transpose(1, 0, 2, 3)
    first = parts.reshape(capacity, devices * stations, 2 * spectra_all)
    second = jnp.concatenate([first[..., spectra_all:], -first[..., :spectra_all]], axis=-1)
    stacked = jnp.stack([first, second], axis=1)
    total = jnp.einsum("cpit,cjt->cpij", stacked, first, preferred_element_type=jnp.float32)
    return total / spectra_all


def solution(mesh):
    return jax.shard_map(
        local,
        mesh=mesh,
        in_specs=(P("chan", "tm", None, None), P(), P(), P()),
        out_specs=P(("chan", "tm"), None, None, None),
        check_vma=False,
    )
```

```python
import functools
import math

import jax
import jax.numpy as jnp
import numpy as np
from jax import lax
from jax.experimental import pallas as pl
from jax.experimental.pallas import tpu as pltpu
from jax.sharding import PartitionSpec as P


def dft_table(channels):
    positions = np.arange(channels, dtype=np.int32)
    phases = positions[:, None] * positions[None, :] % channels
    angles = phases.astype(np.float32) * np.float32(2.0 * math.pi / channels)
    factor = np.float32(1.0 / math.sqrt(channels))
    table = np.concatenate([np.cos(angles) * factor, np.sin(angles) * factor], axis=1)
    return jnp.asarray(table.astype(jnp.bfloat16))


def slot_matrix(flagged, owners, channels, capacity):
    ids = jnp.arange(channels, dtype=jnp.int32)
    alive = jnp.logical_not(jnp.any(flagged[:, None] == ids[None, :], axis=0))
    earlier = (owners[None, :] == owners[:, None]) & alive[None, :] & (ids[None, :] < ids[:, None])
    rank = jnp.sum(earlier.astype(jnp.int32), axis=1)
    slot_of = jnp.where(alive, owners * capacity + rank, -1)
    return (slot_of[None, :] == ids[:, None]).astype(jnp.bfloat16)


GROUP_ROWS = 256
MESH = pl.DeviceIdType.MESH


def turn_kernel(chans, times, halo_ref, fresh_ref, taps_ref, table, picks_ref, order_ref, out_ref, wide, both_ref, spectra, got_ref, sending, send_sem, recv_sem):
    devices = chans * times
    capacity, rows_all = sending.shape[1:]
    channels = table.shape[0]
    stations = out_ref.shape[1]
    halo, spec_dev = halo_ref.shape[0], fresh_ref.shape[0]
    per_group = GROUP_ROWS // capacity
    groups = devices // per_group
    me = lax.axis_index("chan") * times + lax.axis_index("tm")

    barrier = pltpu.get_barrier_semaphore()

    def greet(step, carry):
        other = lax.rem(me + step, devices)
        pl.semaphore_signal(barrier, inc=1, device_id=(other // times, lax.rem(other, times)), device_id_type=MESH)
        return carry

    lax.fori_loop(1, devices, greet, 0)

    def place(source):
        return lax.rem(source, times) * chans + source // times

    def widen(step, carry):
        wide[halo + step] = fresh_ref[step].astype(jnp.float32)
        return carry

    for step in range(halo):
        wide[step] = halo_ref[step].astype(jnp.float32)
    lax.fori_loop(0, spec_dev, widen, 0)
    series = fresh_ref.shape[1]
    real_row = lax.broadcasted_iota(jnp.int32, (series, channels), 0) < series // 2

    def filter_two(step, carry):
        sums, turns = [], []
        for half in range(2):
            total = jnp.zeros((series, channels), jnp.float32)
            for tap in range(halo + 1):
                total = total + taps_ref[pl.ds(tap, 1), :] * wide[2 * step + half + halo - tap]
            swapped = pltpu.roll(total, series // 2, 0)
            sums.append(total)
            turns.append(jnp.where(real_row, swapped, -swapped))
        rows = pl.ds(pl.multiple_of(step * 2 * series, 2 * series), 2 * series)
        both_ref[rows, :channels] = jnp.concatenate(sums, axis=0).astype(jnp.bfloat16)
        both_ref[rows, channels:] = jnp.concatenate(turns, axis=0).astype(jnp.bfloat16)
        return carry

    lax.fori_loop(0, spec_dev // 2, filter_two, 0)

    def block_copy(slot_block, source, other):
        return pltpu.make_async_remote_copy(
            src_ref=sending.at[slot_block],
            dst_ref=got_ref.at[place(source)],
            send_sem=send_sem.at[slot_block],
            recv_sem=recv_sem.at[source],
            device_id=(other // times, lax.rem(other, times)),
            device_id_type=MESH,
        )

    def transform(step, carry):
        rows = pl.ds(pl.multiple_of(step * GROUP_ROWS, GROUP_ROWS), GROUP_ROWS)
        spectra[rows, :] = lax.dot_general(
            table[rows, :], both_ref[...], (((1,), (1,)), ((), ())), preferred_element_type=jnp.float32
        ).astype(jnp.bfloat16)
        return carry

    lax.fori_loop(0, channels // GROUP_ROWS, transform, 0)
    pl.semaphore_wait(barrier, devices - 1)

    def send_group(step, carry):
        group = lax.rem(me // per_group + groups // 2 + step, groups)
        rows = pl.ds(pl.multiple_of(group * GROUP_ROWS, GROUP_ROWS), GROUP_ROWS)
        chosen = jnp.dot(picks_ref[rows, :], spectra[...], preferred_element_type=jnp.float32)
        sending[pl.ds(group * per_group, per_group)] = chosen.astype(jnp.bfloat16).reshape(
            per_group, capacity, chosen.shape[1]
        )

        def send(position, inner):
            other = group * per_group + lax.rem(me + position, per_group)

            @pl.when(other != me)
            def _():
                block_copy(other, me, other).start()

            return inner

        lax.fori_loop(0, per_group, send, 0)
        return carry

    lax.fori_loop(0, groups, send_group, 0)
    got_ref[place(me)] = sending[me]

    def finish(step, carry):
        other = lax.rem(me + step, devices)
        copy = block_copy(other, other, other)
        copy.wait_send()
        copy.wait_recv()
        return carry

    lax.fori_loop(1, devices, finish, 0)

    for station in range(stations):
        total = jnp.zeros((chans * capacity, rows_all), jnp.float32)
        for block in range(times):
            total = total + jnp.dot(
                got_ref[block * chans : (block + 1) * chans].reshape(chans * capacity, rows_all),
                order_ref[block * rows_all : (block + 1) * rows_all, station * rows_all : (station + 1) * rows_all],
                preferred_element_type=jnp.float32,
            )
        out_ref[:, station] = total.astype(jnp.bfloat16).reshape(chans, capacity, rows_all)


def turn(before, fresh, filter_taps, table, picks, order, chans, times, capacity):
    devices = chans * times
    spec_dev, series, channels = fresh.shape
    rows = spec_dev * series
    return pl.pallas_call(
        functools.partial(turn_kernel, chans, times),
        out_shape=jax.ShapeDtypeStruct((chans, series // 2, capacity, rows), jnp.bfloat16),
        in_specs=[pl.BlockSpec(memory_space=pltpu.VMEM)] * 6,
        out_specs=pl.BlockSpec(memory_space=pltpu.VMEM),
        scratch_shapes=[
            pltpu.VMEM((before.shape[0] + spec_dev, series, channels), jnp.float32),
            pltpu.VMEM((rows, 2 * channels), jnp.bfloat16),
            pltpu.VMEM((channels, rows), jnp.bfloat16),
            pltpu.VMEM((devices, capacity, rows), jnp.bfloat16),
            pltpu.VMEM((devices, capacity, rows), jnp.bfloat16),
            pltpu.SemaphoreType.DMA((devices,)),
            pltpu.SemaphoreType.DMA((devices,)),
        ],
        compiler_params=pltpu.CompilerParams(
            collective_id=0, has_side_effects=True, vmem_limit_bytes=32 * 1024 * 1024
        ),
    )(before, fresh, filter_taps, table, picks, order)


def lane_order(stations, spec_dev, blocks):
    shape = (blocks, spec_dev, 2, stations)
    places = np.arange(math.prod(shape)).reshape(shape).transpose(3, 2, 0, 1).reshape(-1)
    table = np.zeros((places.size, places.size), np.float32)
    table[places, np.arange(places.size)] = 1.0
    return jnp.asarray(table.astype(jnp.bfloat16))


def local(voltages, filter_taps, flagged, owners):
    stations, spec_dev, _, channels = voltages.shape
    halo = filter_taps.shape[0] - 1
    chans, times = lax.axis_size("chan"), lax.axis_size("tm")
    devices = chans * times
    capacity = channels // devices
    spectra_all = spec_dev * times
    rows = 2 * stations * spec_dev
    fresh = voltages.transpose(1, 2, 0, 3).reshape(spec_dev, 2 * stations, channels)
    before = lax.ppermute(fresh[spec_dev - halo :], "tm", [(i, i + 1) for i in range(times - 1)])
    picks = slot_matrix(flagged, owners, channels, capacity)
    table = dft_table(channels)
    order = lane_order(stations, spec_dev, times)
    if capacity % 16 == 0 and GROUP_ROWS % capacity == 0 and channels % GROUP_ROWS == 0:
        first = turn(before, fresh, filter_taps, table, picks, order, chans, times, capacity)
        first = first.reshape(chans * stations, capacity, 2 * spectra_all).transpose(1, 0, 2)
    else:
        joined = jnp.concatenate([before, fresh]).astype(jnp.float32)
        running = jnp.zeros(fresh.shape, jnp.float32)
        for tap in range(halo + 1):
            start = halo - tap
            running = running + filter_taps[tap] * joined[start : start + spec_dev]
        turned = jnp.concatenate([running[:, stations:], -running[:, :stations]], axis=1)
        both = jnp.concatenate([running, turned], axis=-1).astype(jnp.bfloat16).reshape(rows, 2 * channels)
        spectra = lax.dot_general(
            table, both, (((1,), (1,)), ((), ())), preferred_element_type=jnp.float32
        ).astype(jnp.bfloat16)
        chosen = jnp.dot(picks, spectra, preferred_element_type=jnp.float32).astype(jnp.bfloat16)
        sending = chosen.reshape(devices, capacity, rows)
        received = lax.all_to_all(sending, ("chan", "tm"), split_axis=0, concat_axis=0, tiled=True)
        parts = received.reshape(chans, times, capacity, rows).transpose(0, 2, 1, 3)
        ordered = jnp.dot(
            parts.reshape(chans * capacity, times * rows), order, preferred_element_type=jnp.float32
        ).astype(jnp.bfloat16)
        first = ordered.reshape(chans, capacity, stations, 2 * spectra_all).transpose(1, 0, 2, 3)
        first = first.reshape(capacity, chans * stations, 2 * spectra_all)
    second = jnp.concatenate([first[..., spectra_all:], -first[..., :spectra_all]], axis=-1)
    stacked = jnp.stack([first, second], axis=1)
    total = jnp.einsum("cpit,cjt->cpij", stacked, first, preferred_element_type=jnp.float32)
    return total / spectra_all


def solution(mesh):
    return jax.shard_map(
        local,
        mesh=mesh,
        in_specs=(P("chan", "tm", None, None), P(), P(), P()),
        out_specs=P(("chan", "tm"), None, None, None),
        check_vma=False,
    )
```

```python
import functools
import math

import jax
import jax.numpy as jnp
import numpy as np
from jax import lax
from jax.experimental import pallas as pl
from jax.experimental.pallas import tpu as pltpu
from jax.sharding import PartitionSpec as P


def dft_table(channels):
    positions = np.arange(channels, dtype=np.int32)
    phases = positions[:, None] * positions[None, :] % channels
    angles = phases.astype(np.float32) * np.float32(2.0 * math.pi / channels)
    factor = np.float32(1.0 / math.sqrt(channels))
    table = np.concatenate([np.cos(angles) * factor, np.sin(angles) * factor], axis=1)
    return jnp.asarray(table.astype(jnp.bfloat16))


def slot_matrix(flagged, owners, channels, capacity):
    ids = jnp.arange(channels, dtype=jnp.int32)
    alive = jnp.logical_not(jnp.any(flagged[:, None] == ids[None, :], axis=0))
    earlier = (owners[None, :] == owners[:, None]) & alive[None, :] & (ids[None, :] < ids[:, None])
    rank = jnp.sum(earlier.astype(jnp.int32), axis=1)
    slot_of = jnp.where(alive, owners * capacity + rank, -1)
    return (slot_of[None, :] == ids[:, None]).astype(jnp.bfloat16)


GROUP_ROWS = 256
MESH = pl.DeviceIdType.MESH


def spread(row):
    return jnp.concatenate(
        [jnp.transpose(jnp.broadcast_to(row[:, i : i + 128], (128, 128))) for i in range(0, row.shape[1], 128)], axis=0
    )


def slot_row(flagged, owners, capacity):
    channels = owners.shape[1]
    owner = owners.astype(jnp.float32)
    marks = spread(flagged.astype(jnp.float32))
    ids = lax.broadcasted_iota(jnp.int32, (1, channels), 1).astype(jnp.float32)
    dead = jnp.concatenate(
        [
            jnp.sum(jnp.where(marks == ids[:, i : i + 128], 1.0, 0.0), axis=0, keepdims=True)
            for i in range(0, channels, 128)
        ],
        axis=1,
    )
    keys = spread(jnp.where(dead > 0.0, -1.0, owner))
    ranks = []
    for i in range(0, channels, 128):
        ahead = keys[: i + 128]
        at = lax.broadcasted_iota(jnp.int32, ahead.shape, 0)
        here = lax.broadcasted_iota(jnp.int32, ahead.shape, 1) + i
        same = (ahead == owner[:, i : i + 128]) & (at < here)
        ranks.append(jnp.sum(jnp.where(same, 1.0, 0.0), axis=0, keepdims=True))
    return jnp.where(dead > 0.0, -1.0, owner * capacity + jnp.concatenate(ranks, axis=1))


def turn_kernel(chans, times, fresh_ref, taps_ref, flagged_ref, owners_ref, table_hbm, order_hbm, out_ref, table, order_ref, halo_ref, wide, both_ref, spectra, got_ref, sending, fetch_sem, halo_sem, send_sem, recv_sem):
    devices = chans * times
    capacity, rows_all = sending.shape[1:]
    channels = table.shape[0]
    stations = out_ref.shape[1]
    halo = taps_ref.shape[0] - 1
    pairs, back = fresh_ref.shape[0], halo_ref.shape[0]
    series = fresh_ref.shape[1] // 2
    chan, time = lax.axis_index("chan"), lax.axis_index("tm")
    fetch_table = pltpu.make_async_copy(table_hbm, table, fetch_sem.at[0])
    fetch_order = pltpu.make_async_copy(order_hbm, order_ref, fetch_sem.at[1])
    fetch_table.start()
    per_group = GROUP_ROWS // capacity
    groups = devices // per_group
    me = lax.axis_index("chan") * times + lax.axis_index("tm")

    barrier = pltpu.get_barrier_semaphore()

    def greet(step, carry):
        other = lax.rem(me + step, devices)
        pl.semaphore_signal(barrier, inc=1, device_id=(other // times, lax.rem(other, times)), device_id_type=MESH)
        return carry

    lax.fori_loop(1, devices, greet, 0)

    def place(source):
        return lax.rem(source, times) * chans + source // times

    def halo_copy(other):
        return pltpu.make_async_remote_copy(
            src_ref=fresh_ref.at[pairs - back :],
            dst_ref=halo_ref,
            send_sem=halo_sem.at[0],
            recv_sem=halo_sem.at[1],
            device_id=(chan, other),
            device_id_type=MESH,
        )

    def widen(pair, where):
        both_times = pair.astype(jnp.float32)
        wide[where] = both_times[:series]
        wide[where + 1] = both_times[series:]

    def widen_fresh(step, carry):
        widen(fresh_ref[step], 2 * (back + step))
        return carry

    lax.fori_loop(0, pairs, widen_fresh, 0)
    pl.semaphore_wait(barrier, devices - 1)

    @pl.when(time < times - 1)
    def _():
        halo_copy(time + 1).start()

    fetch_order.start()
    slots = slot_row(flagged_ref[...], owners_ref[...], capacity)

    @pl.when(time > 0)
    def _():
        halo_copy(time).wait_recv()
        for step in range(back):
            widen(halo_ref[step], 2 * step)

    @pl.when(time == 0)
    def _():
        wide[: 2 * back] = jnp.zeros((2 * back, series, channels), jnp.float32)

    real_row = lax.broadcasted_iota(jnp.int32, (series, channels), 0) < series // 2

    def filter_two(step, carry):
        sums, turns = [], []
        for half in range(2):
            total = jnp.zeros((series, channels), jnp.float32)
            for tap in range(halo + 1):
                total = total + taps_ref[pl.ds(tap, 1), :] * wide[2 * step + half + 2 * back - tap]
            swapped = pltpu.roll(total, series // 2, 0)
            sums.append(total)
            turns.append(jnp.where(real_row, swapped, -swapped))
        rows = pl.ds(pl.multiple_of(step * 2 * series, 2 * series), 2 * series)
        both_ref[rows, :channels] = jnp.concatenate(sums, axis=0).astype(jnp.bfloat16)
        both_ref[rows, channels:] = jnp.concatenate(turns, axis=0).astype(jnp.bfloat16)
        return carry

    lax.fori_loop(0, pairs, filter_two, 0)
    fetch_table.wait()

    def block_copy(slot_block, source, other):
        return pltpu.make_async_remote_copy(
            src_ref=sending.at[slot_block],
            dst_ref=got_ref.at[place(source)],
            send_sem=send_sem.at[slot_block],
            recv_sem=recv_sem.at[source],
            device_id=(other // times, lax.rem(other, times)),
            device_id_type=MESH,
        )

    def transform(step, carry):
        rows = pl.ds(pl.multiple_of(step * GROUP_ROWS, GROUP_ROWS), GROUP_ROWS)
        spectra[rows, :] = lax.dot_general(
            table[rows, :], both_ref[...], (((1,), (1,)), ((), ())), preferred_element_type=jnp.float32
        ).astype(jnp.bfloat16)
        return carry

    lax.fori_loop(0, channels // GROUP_ROWS, transform, 0)

    def send_group(step, carry):
        group = lax.rem(me // per_group + groups // 2 + step, groups)
        held = lax.broadcasted_iota(jnp.int32, (GROUP_ROWS, channels), 0) + group * GROUP_ROWS
        picks = jnp.where(held.astype(jnp.float32) == slots, 1.0, 0.0).astype(jnp.bfloat16)
        chosen = jnp.dot(picks, spectra[...], preferred_element_type=jnp.float32)
        sending[pl.ds(group * per_group, per_group)] = chosen.astype(jnp.bfloat16).reshape(
            per_group, capacity, chosen.shape[1]
        )

        def send(position, inner):
            other = group * per_group + lax.rem(me + position, per_group)

            @pl.when(other != me)
            def _():
                block_copy(other, me, other).start()

            return inner

        lax.fori_loop(0, per_group, send, 0)
        return carry

    lax.fori_loop(0, groups, send_group, 0)
    got_ref[place(me)] = sending[me]

    def finish(step, carry):
        other = lax.rem(me + step, devices)
        copy = block_copy(other, other, other)
        copy.wait_send()
        copy.wait_recv()
        return carry

    lax.fori_loop(1, devices, finish, 0)

    @pl.when(time < times - 1)
    def _():
        halo_copy(time + 1).wait_send()

    fetch_order.wait()
    for station in range(stations):
        total = jnp.zeros((chans * capacity, rows_all), jnp.float32)
        for block in range(times):
            total = total + jnp.dot(
                got_ref[block * chans : (block + 1) * chans].reshape(chans * capacity, rows_all),
                order_ref[block * rows_all : (block + 1) * rows_all, station * rows_all : (station + 1) * rows_all],
                preferred_element_type=jnp.float32,
            )
        out_ref[:, station] = total.astype(jnp.bfloat16).reshape(chans, capacity, rows_all)


def turn(fresh, filter_taps, flagged, owners, table, order, chans, times, capacity):
    devices = chans * times
    pairs, width, channels = fresh.shape
    series = width // 2
    rows = pairs * width
    back = filter_taps.shape[0] // 2
    return pl.pallas_call(
        functools.partial(turn_kernel, chans, times),
        out_shape=jax.ShapeDtypeStruct((chans, series // 2, capacity, rows), jnp.bfloat16),
        in_specs=[pl.BlockSpec(memory_space=pltpu.VMEM)] * 4 + [pl.BlockSpec(memory_space=pl.ANY)] * 2,
        out_specs=pl.BlockSpec(memory_space=pltpu.VMEM),
        scratch_shapes=[
            pltpu.VMEM(table.shape, jnp.bfloat16),
            pltpu.VMEM(order.shape, jnp.bfloat16),
            pltpu.VMEM((back, width, channels), jnp.bfloat16),
            pltpu.VMEM((2 * (back + pairs), series, channels), jnp.float32),
            pltpu.VMEM((rows, 2 * channels), jnp.bfloat16),
            pltpu.VMEM((channels, rows), jnp.bfloat16),
            pltpu.VMEM((devices, capacity, rows), jnp.bfloat16),
            pltpu.VMEM((devices, capacity, rows), jnp.bfloat16),
            pltpu.SemaphoreType.DMA((2,)),
            pltpu.SemaphoreType.DMA((2,)),
            pltpu.SemaphoreType.DMA((devices,)),
            pltpu.SemaphoreType.DMA((devices,)),
        ],
        compiler_params=pltpu.CompilerParams(
            collective_id=0, has_side_effects=True, vmem_limit_bytes=57 * 1024 * 1024
        ),
    )(fresh, filter_taps, flagged.reshape(1, -1), owners.reshape(1, -1), table, order)


def lane_order(stations, spec_dev, blocks):
    shape = (blocks, spec_dev, 2, stations)
    places = np.arange(math.prod(shape)).reshape(shape).transpose(3, 2, 0, 1).reshape(-1)
    table = np.zeros((places.size, places.size), np.float32)
    table[places, np.arange(places.size)] = 1.0
    return jnp.asarray(table.astype(jnp.bfloat16))


def local(voltages, filter_taps, flagged, owners):
    stations, spec_dev, _, channels = voltages.shape
    halo = filter_taps.shape[0] - 1
    chans, times = lax.axis_size("chan"), lax.axis_size("tm")
    devices = chans * times
    capacity = channels // devices
    spectra_all = spec_dev * times
    rows = 2 * stations * spec_dev
    fresh = voltages.transpose(1, 2, 0, 3)
    table = dft_table(channels)
    order = lane_order(stations, spec_dev, times)
    even = halo % 2 == 1 and spec_dev % 2 == 0 and stations % 4 == 0
    if even and capacity % 16 == 0 and GROUP_ROWS % capacity == 0 and channels % GROUP_ROWS == 0:
        paired = fresh.reshape(spec_dev // 2, 4 * stations, channels)
        first = turn(paired, filter_taps, flagged, owners, table, order, chans, times, capacity)
        first = first.reshape(chans * stations, capacity, 2 * spectra_all).transpose(1, 0, 2)
    else:
        fresh = fresh.reshape(spec_dev, 2 * stations, channels)
        before = lax.ppermute(fresh[spec_dev - halo :], "tm", [(i, i + 1) for i in range(times - 1)])
        picks = slot_matrix(flagged, owners, channels, capacity)
        joined = jnp.concatenate([before, fresh]).astype(jnp.float32)
        running = jnp.zeros(fresh.shape, jnp.float32)
        for tap in range(halo + 1):
            start = halo - tap
            running = running + filter_taps[tap] * joined[start : start + spec_dev]
        turned = jnp.concatenate([running[:, stations:], -running[:, :stations]], axis=1)
        both = jnp.concatenate([running, turned], axis=-1).astype(jnp.bfloat16).reshape(rows, 2 * channels)
        spectra = lax.dot_general(
            table, both, (((1,), (1,)), ((), ())), preferred_element_type=jnp.float32
        ).astype(jnp.bfloat16)
        chosen = jnp.dot(picks, spectra, preferred_element_type=jnp.float32).astype(jnp.bfloat16)
        sending = chosen.reshape(devices, capacity, rows)
        received = lax.all_to_all(sending, ("chan", "tm"), split_axis=0, concat_axis=0, tiled=True)
        parts = received.reshape(chans, times, capacity, rows).transpose(0, 2, 1, 3)
        ordered = jnp.dot(
            parts.reshape(chans * capacity, times * rows), order, preferred_element_type=jnp.float32
        ).astype(jnp.bfloat16)
        first = ordered.reshape(chans, capacity, stations, 2 * spectra_all).transpose(1, 0, 2, 3)
        first = first.reshape(capacity, chans * stations, 2 * spectra_all)
    second = jnp.concatenate([first[..., spectra_all:], -first[..., :spectra_all]], axis=-1)
    stacked = jnp.stack([first, second], axis=1)
    total = jnp.einsum("cpit,cjt->cpij", stacked, first, preferred_element_type=jnp.float32)
    return total / spectra_all


def solution(mesh):
    return jax.shard_map(
        local,
        mesh=mesh,
        in_specs=(P("chan", "tm", None, None), P(), P(), P()),
        out_specs=P(("chan", "tm"), None, None, None),
        check_vma=False,
    )
```

```python
import functools
import math

import jax
import jax.numpy as jnp
import numpy as np
from jax import lax
from jax.experimental import pallas as pl
from jax.experimental.pallas import tpu as pltpu
from jax.sharding import PartitionSpec as P


def dft_table(channels):
    positions = np.arange(channels, dtype=np.int32)
    phases = positions[:, None] * positions[None, :] % channels
    angles = phases.astype(np.float32) * np.float32(2.0 * math.pi / channels)
    factor = np.float32(1.0 / math.sqrt(channels))
    table = np.concatenate([np.cos(angles) * factor, np.sin(angles) * factor], axis=1)
    return jnp.asarray(table.astype(jnp.bfloat16))


def slot_matrix(flagged, owners, channels, capacity):
    ids = jnp.arange(channels, dtype=jnp.int32)
    alive = jnp.logical_not(jnp.any(flagged[:, None] == ids[None, :], axis=0))
    earlier = (owners[None, :] == owners[:, None]) & alive[None, :] & (ids[None, :] < ids[:, None])
    rank = jnp.sum(earlier.astype(jnp.int32), axis=1)
    slot_of = jnp.where(alive, owners * capacity + rank, -1)
    return (slot_of[None, :] == ids[:, None]).astype(jnp.bfloat16)


GROUP_ROWS = 256
MESH = pl.DeviceIdType.MESH


def spread(row):
    return jnp.concatenate(
        [jnp.transpose(jnp.broadcast_to(row[:, i : i + 128], (128, 128))) for i in range(0, row.shape[1], 128)], axis=0
    )


def slot_row(flagged, owners, capacity):
    channels = owners.shape[1]
    owner = owners.astype(jnp.float32)
    marks = spread(flagged.astype(jnp.float32))
    ids = lax.broadcasted_iota(jnp.int32, (1, channels), 1).astype(jnp.float32)
    dead = jnp.concatenate(
        [
            jnp.sum(jnp.where(marks == ids[:, i : i + 128], 1.0, 0.0), axis=0, keepdims=True)
            for i in range(0, channels, 128)
        ],
        axis=1,
    )
    keys = spread(jnp.where(dead > 0.0, -1.0, owner))
    ranks = []
    for i in range(0, channels, 128):
        ahead = keys[: i + 128]
        at = lax.broadcasted_iota(jnp.int32, ahead.shape, 0)
        here = lax.broadcasted_iota(jnp.int32, ahead.shape, 1) + i
        same = (ahead == owner[:, i : i + 128]) & (at < here)
        ranks.append(jnp.sum(jnp.where(same, 1.0, 0.0), axis=0, keepdims=True))
    return jnp.where(dead > 0.0, -1.0, owner * capacity + jnp.concatenate(ranks, axis=1))


def turn_kernel(chans, times, fresh_ref, taps_ref, flagged_ref, owners_ref, table_hbm, order_hbm, out_ref, table, order_ref, halo_ref, wide, both_ref, spectra, got_ref, sending, fetch_sem, halo_sem, send_sem, recv_sem):
    devices = chans * times
    capacity, rows_all = sending.shape[1:]
    channels = table.shape[0]
    stations = out_ref.shape[1]
    halo = taps_ref.shape[0] - 1
    pairs, back = fresh_ref.shape[0], halo_ref.shape[0]
    series = fresh_ref.shape[1] // 2
    chan, time = lax.axis_index("chan"), lax.axis_index("tm")
    fetch_table = pltpu.make_async_copy(table_hbm, table, fetch_sem.at[0])
    fetch_order = pltpu.make_async_copy(order_hbm, order_ref, fetch_sem.at[1])
    fetch_table.start()
    per_group = GROUP_ROWS // capacity
    groups = devices // per_group
    me = lax.axis_index("chan") * times + lax.axis_index("tm")

    barrier = pltpu.get_barrier_semaphore()

    def greet(step, carry):
        other = lax.rem(me + step, devices)
        pl.semaphore_signal(barrier, inc=1, device_id=(other // times, lax.rem(other, times)), device_id_type=MESH)
        return carry

    lax.fori_loop(1, devices, greet, 0)

    def place(source):
        return lax.rem(source, times) * chans + source // times

    def halo_copy(other):
        return pltpu.make_async_remote_copy(
            src_ref=fresh_ref.at[pairs - back :],
            dst_ref=halo_ref,
            send_sem=halo_sem.at[0],
            recv_sem=halo_sem.at[1],
            device_id=(chan, other),
            device_id_type=MESH,
        )

    def widen(pair, where):
        both_times = pair.astype(jnp.float32)
        wide[where] = both_times[:series]
        wide[where + 1] = both_times[series:]

    def widen_fresh(step, carry):
        widen(fresh_ref[step], 2 * (back + step))
        return carry

    lax.fori_loop(0, pairs, widen_fresh, 0)
    pl.semaphore_wait(barrier, devices - 1)

    @pl.when(time < times - 1)
    def _():
        halo_copy(time + 1).start()

    fetch_order.start()
    slots = slot_row(flagged_ref[...], owners_ref[...], capacity)

    @pl.when(time > 0)
    def _():
        halo_copy(time).wait_recv()
        for step in range(back):
            widen(halo_ref[step], 2 * step)

    @pl.when(time == 0)
    def _():
        wide[: 2 * back] = jnp.zeros((2 * back, series, channels), jnp.float32)

    real_row = lax.broadcasted_iota(jnp.int32, (series, channels), 0) < series // 2

    def filter_two(step, carry):
        sums, turns = [], []
        for half in range(2):
            total = jnp.zeros((series, channels), jnp.float32)
            for tap in range(halo + 1):
                total = total + taps_ref[pl.ds(tap, 1), :] * wide[2 * step + half + 2 * back - tap]
            swapped = pltpu.roll(total, series // 2, 0)
            sums.append(total)
            turns.append(jnp.where(real_row, swapped, -swapped))
        rows = pl.ds(pl.multiple_of(step * 2 * series, 2 * series), 2 * series)
        both_ref[rows, :channels] = jnp.concatenate(sums, axis=0).astype(jnp.bfloat16)
        both_ref[rows, channels:] = jnp.concatenate(turns, axis=0).astype(jnp.bfloat16)
        return carry

    lax.fori_loop(0, pairs, filter_two, 0)
    fetch_table.wait()

    def block_copy(slot_block, source, other):
        return pltpu.make_async_remote_copy(
            src_ref=sending.at[slot_block],
            dst_ref=got_ref.at[place(source)],
            send_sem=send_sem.at[slot_block],
            recv_sem=recv_sem.at[source],
            device_id=(other // times, lax.rem(other, times)),
            device_id_type=MESH,
        )

    def transform(step, carry):
        rows = pl.ds(pl.multiple_of(step * GROUP_ROWS, GROUP_ROWS), GROUP_ROWS)
        spectra[rows, :] = lax.dot_general(
            table[rows, :], both_ref[...], (((1,), (1,)), ((), ())), preferred_element_type=jnp.float32
        ).astype(jnp.bfloat16)
        return carry

    lax.fori_loop(0, channels // GROUP_ROWS, transform, 0)

    def send_group(step, carry):
        group = lax.rem(me // per_group + groups // 2 + step, groups)
        held = lax.broadcasted_iota(jnp.int32, (GROUP_ROWS, channels), 0) + group * GROUP_ROWS
        picks = jnp.where(held.astype(jnp.float32) == slots, 1.0, 0.0).astype(jnp.bfloat16)
        chosen = jnp.dot(picks, spectra[...], preferred_element_type=jnp.float32)
        sending[pl.ds(group * per_group, per_group)] = chosen.astype(jnp.bfloat16).reshape(
            per_group, capacity, chosen.shape[1]
        )

        def send(position, inner):
            other = group * per_group + lax.rem(me + position, per_group)

            @pl.when(other != me)
            def _():
                block_copy(other, me, other).start()

            return inner

        lax.fori_loop(0, per_group, send, 0)
        return carry

    lax.fori_loop(0, groups, send_group, 0)
    got_ref[place(me)] = sending[me]

    def finish(step, carry):
        other = lax.rem(me + step, devices)
        copy = block_copy(other, other, other)
        copy.wait_send()
        copy.wait_recv()
        return carry

    lax.fori_loop(1, devices, finish, 0)

    @pl.when(time < times - 1)
    def _():
        halo_copy(time + 1).wait_send()

    fetch_order.wait()
    for station in range(stations):
        total = jnp.zeros((chans * capacity, rows_all), jnp.float32)
        for block in range(times):
            total = total + jnp.dot(
                got_ref[block * chans : (block + 1) * chans].reshape(chans * capacity, rows_all),
                order_ref[block * rows_all : (block + 1) * rows_all, station * rows_all : (station + 1) * rows_all],
                preferred_element_type=jnp.float32,
            )
        out_ref[:, station] = total.astype(jnp.bfloat16).reshape(chans, capacity, rows_all)


def turn(fresh, filter_taps, flagged, owners, table, order, chans, times, capacity):
    devices = chans * times
    pairs, width, channels = fresh.shape
    series = width // 2
    rows = pairs * width
    back = filter_taps.shape[0] // 2
    return pl.pallas_call(
        functools.partial(turn_kernel, chans, times),
        out_shape=jax.ShapeDtypeStruct((chans, series // 2, capacity, rows), jnp.bfloat16),
        in_specs=[pl.BlockSpec(memory_space=pltpu.VMEM)] * 4 + [pl.BlockSpec(memory_space=pl.ANY)] * 2,
        out_specs=pl.BlockSpec(memory_space=pltpu.VMEM),
        scratch_shapes=[
            pltpu.VMEM(table.shape, jnp.bfloat16),
            pltpu.VMEM(order.shape, jnp.bfloat16),
            pltpu.VMEM((back, width, channels), jnp.bfloat16),
            pltpu.VMEM((2 * (back + pairs), series, channels), jnp.float32),
            pltpu.VMEM((rows, 2 * channels), jnp.bfloat16),
            pltpu.VMEM((channels, rows), jnp.bfloat16),
            pltpu.VMEM((devices, capacity, rows), jnp.bfloat16),
            pltpu.VMEM((devices, capacity, rows), jnp.bfloat16),
            pltpu.SemaphoreType.DMA((2,)),
            pltpu.SemaphoreType.DMA((2,)),
            pltpu.SemaphoreType.DMA((devices,)),
            pltpu.SemaphoreType.DMA((devices,)),
        ],
        compiler_params=pltpu.CompilerParams(
            collective_id=0, has_side_effects=True, vmem_limit_bytes=52 * 1024 * 1024
        ),
    )(fresh, filter_taps, flagged.reshape(1, -1), owners.reshape(1, -1), table, order)


def lane_order(stations, spec_dev, blocks):
    shape = (blocks, spec_dev, 2, stations)
    places = np.arange(math.prod(shape)).reshape(shape).transpose(3, 2, 0, 1).reshape(-1)
    table = np.zeros((places.size, places.size), np.float32)
    table[places, np.arange(places.size)] = 1.0
    return jnp.asarray(table.astype(jnp.bfloat16))


def local(voltages, filter_taps, flagged, owners):
    stations, spec_dev, _, channels = voltages.shape
    halo = filter_taps.shape[0] - 1
    chans, times = lax.axis_size("chan"), lax.axis_size("tm")
    devices = chans * times
    capacity = channels // devices
    spectra_all = spec_dev * times
    rows = 2 * stations * spec_dev
    fresh = voltages.transpose(1, 2, 0, 3)
    table = dft_table(channels)
    order = lane_order(stations, spec_dev, times)
    even = halo % 2 == 1 and spec_dev % 2 == 0 and stations % 4 == 0
    if even and capacity % 16 == 0 and GROUP_ROWS % capacity == 0 and channels % GROUP_ROWS == 0:
        paired = fresh.reshape(spec_dev // 2, 4 * stations, channels)
        first = turn(paired, filter_taps, flagged, owners, table, order, chans, times, capacity)
        first = first.reshape(chans * stations, capacity, 2 * spectra_all).transpose(1, 0, 2)
    else:
        fresh = fresh.reshape(spec_dev, 2 * stations, channels)
        before = lax.ppermute(fresh[spec_dev - halo :], "tm", [(i, i + 1) for i in range(times - 1)])
        picks = slot_matrix(flagged, owners, channels, capacity)
        joined = jnp.concatenate([before, fresh]).astype(jnp.float32)
        running = jnp.zeros(fresh.shape, jnp.float32)
        for tap in range(halo + 1):
            start = halo - tap
            running = running + filter_taps[tap] * joined[start : start + spec_dev]
        turned = jnp.concatenate([running[:, stations:], -running[:, :stations]], axis=1)
        both = jnp.concatenate([running, turned], axis=-1).astype(jnp.bfloat16).reshape(rows, 2 * channels)
        spectra = lax.dot_general(
            table, both, (((1,), (1,)), ((), ())), preferred_element_type=jnp.float32
        ).astype(jnp.bfloat16)
        chosen = jnp.dot(picks, spectra, preferred_element_type=jnp.float32).astype(jnp.bfloat16)
        sending = chosen.reshape(devices, capacity, rows)
        received = lax.all_to_all(sending, ("chan", "tm"), split_axis=0, concat_axis=0, tiled=True)
        parts = received.reshape(chans, times, capacity, rows).transpose(0, 2, 1, 3)
        ordered = jnp.dot(
            parts.reshape(chans * capacity, times * rows), order, preferred_element_type=jnp.float32
        ).astype(jnp.bfloat16)
        first = ordered.reshape(chans, capacity, stations, 2 * spectra_all).transpose(1, 0, 2, 3)
        first = first.reshape(capacity, chans * stations, 2 * spectra_all)
    second = jnp.concatenate([first[..., spectra_all:], -first[..., :spectra_all]], axis=-1)
    stacked = jnp.stack([first, second], axis=1)
    total = jnp.einsum("cpit,cjt->cpij", stacked, first, preferred_element_type=jnp.float32)
    return total / spectra_all


def solution(mesh):
    return jax.shard_map(
        local,
        mesh=mesh,
        in_specs=(P("chan", "tm", None, None), P(), P(), P()),
        out_specs=P(("chan", "tm"), None, None, None),
        check_vma=False,
    )
```

```python
import functools
import math

import jax
import jax.numpy as jnp
import numpy as np
from jax import lax
from jax.experimental import pallas as pl
from jax.experimental.pallas import tpu as pltpu
from jax.sharding import PartitionSpec as P


def dft_table(channels):
    positions = np.arange(channels, dtype=np.int32)
    phases = positions[:, None] * positions[None, :] % channels
    angles = phases.astype(np.float32) * np.float32(2.0 * math.pi / channels)
    factor = np.float32(1.0 / math.sqrt(channels))
    table = np.concatenate([np.cos(angles) * factor, np.sin(angles) * factor], axis=1)
    return jnp.asarray(table.astype(jnp.bfloat16))


def slot_matrix(flagged, owners, channels, capacity):
    ids = jnp.arange(channels, dtype=jnp.int32)
    alive = jnp.logical_not(jnp.any(flagged[:, None] == ids[None, :], axis=0))
    earlier = (owners[None, :] == owners[:, None]) & alive[None, :] & (ids[None, :] < ids[:, None])
    rank = jnp.sum(earlier.astype(jnp.int32), axis=1)
    slot_of = jnp.where(alive, owners * capacity + rank, -1)
    return (slot_of[None, :] == ids[:, None]).astype(jnp.bfloat16)


GROUP_ROWS = 256
MESH = pl.DeviceIdType.MESH


def spread(row):
    return jnp.concatenate(
        [jnp.transpose(jnp.broadcast_to(row[:, i : i + 128], (128, 128))) for i in range(0, row.shape[1], 128)], axis=0
    )


def slot_row(flagged, owners, capacity):
    channels = owners.shape[1]
    owner = owners
    marks = spread(flagged)
    ids = lax.broadcasted_iota(jnp.int32, (1, channels), 1).astype(jnp.float32)
    dead = jnp.concatenate(
        [
            jnp.sum(jnp.where(marks == ids[:, i : i + 128], 1.0, 0.0), axis=0, keepdims=True)
            for i in range(0, channels, 128)
        ],
        axis=1,
    )
    keys = spread(jnp.where(dead > 0.0, -1.0, owner))
    ranks = []
    for i in range(0, channels, 128):
        ahead = keys[: i + 128]
        at = lax.broadcasted_iota(jnp.int32, ahead.shape, 0)
        here = lax.broadcasted_iota(jnp.int32, ahead.shape, 1) + i
        same = (ahead == owner[:, i : i + 128]) & (at < here)
        ranks.append(jnp.sum(jnp.where(same, 1.0, 0.0), axis=0, keepdims=True))
    return jnp.where(dead > 0.0, -1.0, owner * capacity + jnp.concatenate(ranks, axis=1))


def turn_kernel(chans, times, flags, fresh_ref, taps_ref, table_hbm, order_hbm, out_ref, table, order_ref, halo_ref, wide, both_ref, spectra, got_ref, sending, fetch_sem, halo_sem, send_sem, recv_sem):
    devices = chans * times
    capacity, rows_all = sending.shape[1:]
    channels = table.shape[0]
    stations = out_ref.shape[1]
    taps = taps_ref.shape[0] - 2
    halo = taps - 1
    pairs, back = fresh_ref.shape[0], halo_ref.shape[0]
    series = fresh_ref.shape[1] // 2
    chan, time = lax.axis_index("chan"), lax.axis_index("tm")
    fetch_table = pltpu.make_async_copy(table_hbm, table, fetch_sem.at[0])
    fetch_order = pltpu.make_async_copy(order_hbm, order_ref, fetch_sem.at[1])
    fetch_table.start()
    per_group = GROUP_ROWS // capacity
    groups = devices // per_group
    me = lax.axis_index("chan") * times + lax.axis_index("tm")

    barrier = pltpu.get_barrier_semaphore()

    def greet(step, carry):
        other = lax.rem(me + step, devices)
        pl.semaphore_signal(barrier, inc=1, device_id=(other // times, lax.rem(other, times)), device_id_type=MESH)
        return carry

    lax.fori_loop(1, devices, greet, 0)

    def place(source):
        return lax.rem(source, times) * chans + source // times

    def halo_copy(other):
        return pltpu.make_async_remote_copy(
            src_ref=fresh_ref.at[pairs - back :],
            dst_ref=halo_ref,
            send_sem=halo_sem.at[0],
            recv_sem=halo_sem.at[1],
            device_id=(chan, other),
            device_id_type=MESH,
        )

    def widen(pair, where):
        both_times = pair.astype(jnp.float32)
        wide[where] = both_times[:series]
        wide[where + 1] = both_times[series:]

    def widen_fresh(step, carry):
        widen(fresh_ref[step], 2 * (back + step))
        return carry

    lax.fori_loop(0, pairs, widen_fresh, 0)
    pl.semaphore_wait(barrier, devices - 1)

    @pl.when(time < times - 1)
    def _():
        halo_copy(time + 1).start()

    fetch_order.start()
    slots = slot_row(taps_ref[taps + 1 : taps + 2, :flags], taps_ref[taps : taps + 1, :], capacity)

    @pl.when(time > 0)
    def _():
        halo_copy(time).wait_recv()
        for step in range(back):
            widen(halo_ref[step], 2 * step)

    @pl.when(time == 0)
    def _():
        wide[: 2 * back] = jnp.zeros((2 * back, series, channels), jnp.float32)

    real_row = lax.broadcasted_iota(jnp.int32, (series, channels), 0) < series // 2

    def filter_two(step, carry):
        sums, turns = [], []
        for half in range(2):
            total = jnp.zeros((series, channels), jnp.float32)
            for tap in range(halo + 1):
                total = total + taps_ref[pl.ds(tap, 1), :] * wide[2 * step + half + 2 * back - tap]
            swapped = pltpu.roll(total, series // 2, 0)
            sums.append(total)
            turns.append(jnp.where(real_row, swapped, -swapped))
        rows = pl.ds(pl.multiple_of(step * 2 * series, 2 * series), 2 * series)
        both_ref[rows, :channels] = jnp.concatenate(sums, axis=0).astype(jnp.bfloat16)
        both_ref[rows, channels:] = jnp.concatenate(turns, axis=0).astype(jnp.bfloat16)
        return carry

    lax.fori_loop(0, pairs, filter_two, 0)
    fetch_table.wait()

    def block_copy(slot_block, source, other):
        return pltpu.make_async_remote_copy(
            src_ref=sending.at[slot_block],
            dst_ref=got_ref.at[place(source)],
            send_sem=send_sem.at[slot_block],
            recv_sem=recv_sem.at[source],
            device_id=(other // times, lax.rem(other, times)),
            device_id_type=MESH,
        )

    def transform(step, carry):
        rows = pl.ds(pl.multiple_of(step * GROUP_ROWS, GROUP_ROWS), GROUP_ROWS)
        spectra[rows, :] = lax.dot_general(
            table[rows, :], both_ref[...], (((1,), (1,)), ((), ())), preferred_element_type=jnp.float32
        ).astype(jnp.bfloat16)
        return carry

    lax.fori_loop(0, channels // GROUP_ROWS, transform, 0)

    def send_group(step, carry):
        group = lax.rem(me // per_group + groups // 2 + step, groups)
        held = lax.broadcasted_iota(jnp.int32, (GROUP_ROWS, channels), 0) + group * GROUP_ROWS
        picks = jnp.where(held.astype(jnp.float32) == slots, 1.0, 0.0).astype(jnp.bfloat16)
        chosen = jnp.dot(picks, spectra[...], preferred_element_type=jnp.float32)
        sending[pl.ds(group * per_group, per_group)] = chosen.astype(jnp.bfloat16).reshape(
            per_group, capacity, chosen.shape[1]
        )

        def send(position, inner):
            other = group * per_group + lax.rem(me + position, per_group)

            @pl.when(other != me)
            def _():
                block_copy(other, me, other).start()

            return inner

        lax.fori_loop(0, per_group, send, 0)
        return carry

    lax.fori_loop(0, groups, send_group, 0)
    got_ref[place(me)] = sending[me]

    def finish(step, carry):
        other = lax.rem(me + step, devices)
        copy = block_copy(other, other, other)
        copy.wait_send()
        copy.wait_recv()
        return carry

    lax.fori_loop(1, devices, finish, 0)

    @pl.when(time < times - 1)
    def _():
        halo_copy(time + 1).wait_send()

    fetch_order.wait()
    for station in range(stations):
        total = jnp.zeros((chans * capacity, rows_all), jnp.float32)
        for block in range(times):
            total = total + jnp.dot(
                got_ref[block * chans : (block + 1) * chans].reshape(chans * capacity, rows_all),
                order_ref[block * rows_all : (block + 1) * rows_all, station * rows_all : (station + 1) * rows_all],
                preferred_element_type=jnp.float32,
            )
        out_ref[:, station] = total.astype(jnp.bfloat16).reshape(chans, capacity, rows_all)


def turn(fresh, filter_taps, flagged, owners, table, order, chans, times, capacity):
    devices = chans * times
    pairs, width, channels = fresh.shape
    series = width // 2
    rows = pairs * width
    back = filter_taps.shape[0] // 2
    flags = jnp.pad(flagged, (0, channels - flagged.size))
    small = jnp.concatenate([filter_taps, owners.astype(jnp.float32)[None], flags.astype(jnp.float32)[None]])
    return pl.pallas_call(
        functools.partial(turn_kernel, chans, times, flagged.size),
        out_shape=jax.ShapeDtypeStruct((chans, series // 2, capacity, rows), jnp.bfloat16),
        in_specs=[pl.BlockSpec(memory_space=pltpu.VMEM)] * 2 + [pl.BlockSpec(memory_space=pl.ANY)] * 2,
        out_specs=pl.BlockSpec(memory_space=pltpu.VMEM),
        scratch_shapes=[
            pltpu.VMEM(table.shape, jnp.bfloat16),
            pltpu.VMEM(order.shape, jnp.bfloat16),
            pltpu.VMEM((back, width, channels), jnp.bfloat16),
            pltpu.VMEM((2 * (back + pairs), series, channels), jnp.float32),
            pltpu.VMEM((rows, 2 * channels), jnp.bfloat16),
            pltpu.VMEM((channels, rows), jnp.bfloat16),
            pltpu.VMEM((devices, capacity, rows), jnp.bfloat16),
            pltpu.VMEM((devices, capacity, rows), jnp.bfloat16),
            pltpu.SemaphoreType.DMA((2,)),
            pltpu.SemaphoreType.DMA((2,)),
            pltpu.SemaphoreType.DMA((devices,)),
            pltpu.SemaphoreType.DMA((devices,)),
        ],
        compiler_params=pltpu.CompilerParams(
            collective_id=0, has_side_effects=True, vmem_limit_bytes=52 * 1024 * 1024
        ),
    )(fresh, small, table, order)


def lane_order(stations, spec_dev, blocks):
    shape = (blocks, spec_dev, 2, stations)
    places = np.arange(math.prod(shape)).reshape(shape).transpose(3, 2, 0, 1).reshape(-1)
    table = np.zeros((places.size, places.size), np.float32)
    table[places, np.arange(places.size)] = 1.0
    return jnp.asarray(table.astype(jnp.bfloat16))


def local(voltages, filter_taps, flagged, owners):
    stations, spec_dev, _, channels = voltages.shape
    halo = filter_taps.shape[0] - 1
    chans, times = lax.axis_size("chan"), lax.axis_size("tm")
    devices = chans * times
    capacity = channels // devices
    spectra_all = spec_dev * times
    rows = 2 * stations * spec_dev
    fresh = voltages.transpose(1, 2, 0, 3)
    table = dft_table(channels)
    order = lane_order(stations, spec_dev, times)
    even = halo % 2 == 1 and spec_dev % 2 == 0 and stations % 4 == 0
    if even and capacity % 16 == 0 and GROUP_ROWS % capacity == 0 and channels % GROUP_ROWS == 0:
        paired = fresh.reshape(spec_dev // 2, 4 * stations, channels)
        first = turn(paired, filter_taps, flagged, owners, table, order, chans, times, capacity)
        first = first.reshape(chans * stations, capacity, 2 * spectra_all).transpose(1, 0, 2)
    else:
        fresh = fresh.reshape(spec_dev, 2 * stations, channels)
        before = lax.ppermute(fresh[spec_dev - halo :], "tm", [(i, i + 1) for i in range(times - 1)])
        picks = slot_matrix(flagged, owners, channels, capacity)
        joined = jnp.concatenate([before, fresh]).astype(jnp.float32)
        running = jnp.zeros(fresh.shape, jnp.float32)
        for tap in range(halo + 1):
            start = halo - tap
            running = running + filter_taps[tap] * joined[start : start + spec_dev]
        turned = jnp.concatenate([running[:, stations:], -running[:, :stations]], axis=1)
        both = jnp.concatenate([running, turned], axis=-1).astype(jnp.bfloat16).reshape(rows, 2 * channels)
        spectra = lax.dot_general(
            table, both, (((1,), (1,)), ((), ())), preferred_element_type=jnp.float32
        ).astype(jnp.bfloat16)
        chosen = jnp.dot(picks, spectra, preferred_element_type=jnp.float32).astype(jnp.bfloat16)
        sending = chosen.reshape(devices, capacity, rows)
        received = lax.all_to_all(sending, ("chan", "tm"), split_axis=0, concat_axis=0, tiled=True)
        parts = received.reshape(chans, times, capacity, rows).transpose(0, 2, 1, 3)
        ordered = jnp.dot(
            parts.reshape(chans * capacity, times * rows), order, preferred_element_type=jnp.float32
        ).astype(jnp.bfloat16)
        first = ordered.reshape(chans, capacity, stations, 2 * spectra_all).transpose(1, 0, 2, 3)
        first = first.reshape(capacity, chans * stations, 2 * spectra_all)
    second = jnp.concatenate([first[..., spectra_all:], -first[..., :spectra_all]], axis=-1)
    stacked = jnp.stack([first, second], axis=1)
    total = jnp.einsum("cpit,cjt->cpij", stacked, first, preferred_element_type=jnp.float32)
    return total / spectra_all


def solution(mesh):
    return jax.shard_map(
        local,
        mesh=mesh,
        in_specs=(P("chan", "tm", None, None), P(), P(), P()),
        out_specs=P(("chan", "tm"), None, None, None),
        check_vma=False,
    )
```

```python
import functools
import math

import jax
import jax.numpy as jnp
import numpy as np
from jax import lax
from jax.experimental import pallas as pl
from jax.experimental.pallas import tpu as pltpu
from jax.sharding import PartitionSpec as P


def dft_table(channels):
    positions = np.arange(channels, dtype=np.int32)
    phases = positions[:, None] * positions[None, :] % channels
    angles = phases.astype(np.float32) * np.float32(2.0 * math.pi / channels)
    factor = np.float32(1.0 / math.sqrt(channels))
    table = np.concatenate([np.cos(angles) * factor, np.sin(angles) * factor], axis=1)
    return jnp.asarray(table.astype(jnp.bfloat16))


def slot_matrix(flagged, owners, channels, capacity):
    ids = jnp.arange(channels, dtype=jnp.int32)
    alive = jnp.logical_not(jnp.any(flagged[:, None] == ids[None, :], axis=0))
    earlier = (owners[None, :] == owners[:, None]) & alive[None, :] & (ids[None, :] < ids[:, None])
    rank = jnp.sum(earlier.astype(jnp.int32), axis=1)
    slot_of = jnp.where(alive, owners * capacity + rank, -1)
    return (slot_of[None, :] == ids[:, None]).astype(jnp.bfloat16)


GROUP_ROWS = 256
MESH = pl.DeviceIdType.MESH


def spread(row):
    return jnp.concatenate(
        [jnp.transpose(jnp.broadcast_to(row[:, i : i + 128], (128, 128))) for i in range(0, row.shape[1], 128)], axis=0
    )


def slot_row(flagged, owners, capacity):
    channels = owners.shape[1]
    owner = owners.astype(jnp.float32)
    marks = spread(flagged.astype(jnp.float32))
    ids = lax.broadcasted_iota(jnp.int32, (1, channels), 1).astype(jnp.float32)
    dead = jnp.concatenate(
        [
            jnp.sum(jnp.where(marks == ids[:, i : i + 128], 1.0, 0.0), axis=0, keepdims=True)
            for i in range(0, channels, 128)
        ],
        axis=1,
    )
    keys = spread(jnp.where(dead > 0.0, -1.0, owner))
    ranks = []
    for i in range(0, channels, 128):
        ahead = keys[: i + 128]
        at = lax.broadcasted_iota(jnp.int32, ahead.shape, 0)
        here = lax.broadcasted_iota(jnp.int32, ahead.shape, 1) + i
        same = (ahead == owner[:, i : i + 128]) & (at < here)
        ranks.append(jnp.sum(jnp.where(same, 1.0, 0.0), axis=0, keepdims=True))
    return jnp.where(dead > 0.0, -1.0, owner * capacity + jnp.concatenate(ranks, axis=1))


def turn_kernel(chans, times, fresh_ref, taps_ref, flagged_ref, owners_ref, table_hbm, order_hbm, out_ref, table, order_ref, halo_ref, wide, both_ref, spectra, got_ref, sending, fetch_sem, halo_sem, send_sem, recv_sem):
    devices = chans * times
    capacity, rows_all = sending.shape[1:]
    channels = table.shape[0]
    stations = out_ref.shape[1]
    halo = taps_ref.shape[0] - 1
    pairs, back = fresh_ref.shape[0], halo_ref.shape[0]
    series = fresh_ref.shape[1] // 2
    chan, time = lax.axis_index("chan"), lax.axis_index("tm")
    fetch_table = pltpu.make_async_copy(table_hbm, table, fetch_sem.at[0])
    fetch_order = pltpu.make_async_copy(order_hbm, order_ref, fetch_sem.at[1])
    fetch_table.start()
    per_group = GROUP_ROWS // capacity
    groups = devices // per_group
    me = lax.axis_index("chan") * times + lax.axis_index("tm")

    barrier = pltpu.get_barrier_semaphore()

    def greet(step, carry):
        other = lax.rem(me + step, devices)
        pl.semaphore_signal(barrier, inc=1, device_id=(other // times, lax.rem(other, times)), device_id_type=MESH)
        return carry

    lax.fori_loop(1, devices, greet, 0)

    def place(source):
        return lax.rem(source, times) * chans + source // times

    def halo_copy(other):
        return pltpu.make_async_remote_copy(
            src_ref=fresh_ref.at[pairs - back :],
            dst_ref=halo_ref,
            send_sem=halo_sem.at[0],
            recv_sem=halo_sem.at[1],
            device_id=(chan, other),
            device_id_type=MESH,
        )

    def widen(pair, where):
        both_times = pair.astype(jnp.float32)
        wide[where] = both_times[:series]
        wide[where + 1] = both_times[series:]

    def widen_fresh(step, carry):
        widen(fresh_ref[step], 2 * (back + step))
        return carry

    lax.fori_loop(0, pairs, widen_fresh, 0)
    pl.semaphore_wait(barrier, devices - 1)

    @pl.when(time < times - 1)
    def _():
        halo_copy(time + 1).start()

    fetch_order.start()
    slots = slot_row(flagged_ref[...], owners_ref[...], capacity)

    @pl.when(time > 0)
    def _():
        halo_copy(time).wait_recv()
        for step in range(back):
            widen(halo_ref[step], 2 * step)

    @pl.when(time == 0)
    def _():
        wide[: 2 * back] = jnp.zeros((2 * back, series, channels), jnp.float32)

    real_row = lax.broadcasted_iota(jnp.int32, (series, channels), 0) < series // 2

    def filter_two(step, carry):
        sums, turns = [], []
        for half in range(2):
            total = jnp.zeros((series, channels), jnp.float32)
            for tap in range(halo + 1):
                total = total + taps_ref[pl.ds(tap, 1), :] * wide[2 * step + half + 2 * back - tap]
            swapped = pltpu.roll(total, series // 2, 0)
            sums.append(total)
            turns.append(jnp.where(real_row, swapped, -swapped))
        rows = pl.ds(pl.multiple_of(step * 2 * series, 2 * series), 2 * series)
        both_ref[rows, :channels] = jnp.concatenate(sums, axis=0).astype(jnp.bfloat16)
        both_ref[rows, channels:] = jnp.concatenate(turns, axis=0).astype(jnp.bfloat16)
        return carry

    lax.fori_loop(0, pairs, filter_two, 0)
    fetch_table.wait()

    def block_copy(slot_block, source, other):
        return pltpu.make_async_remote_copy(
            src_ref=sending.at[slot_block],
            dst_ref=got_ref.at[place(source)],
            send_sem=send_sem.at[slot_block],
            recv_sem=recv_sem.at[source],
            device_id=(other // times, lax.rem(other, times)),
            device_id_type=MESH,
        )

    def transform(step, carry):
        rows = pl.ds(pl.multiple_of(step * GROUP_ROWS, GROUP_ROWS), GROUP_ROWS)
        spectra[rows, :] = lax.dot_general(
            table[rows, :], both_ref[...], (((1,), (1,)), ((), ())), preferred_element_type=jnp.float32
        ).astype(jnp.bfloat16)
        return carry

    lax.fori_loop(0, channels // GROUP_ROWS, transform, 0)

    def send_group(step, carry):
        group = lax.rem(me // per_group + groups - 1 - step, groups)
        held = lax.broadcasted_iota(jnp.int32, (GROUP_ROWS, channels), 0) + group * GROUP_ROWS
        picks = jnp.where(held.astype(jnp.float32) == slots, 1.0, 0.0).astype(jnp.bfloat16)
        chosen = jnp.dot(picks, spectra[...], preferred_element_type=jnp.float32)
        sending[pl.ds(group * per_group, per_group)] = chosen.astype(jnp.bfloat16).reshape(
            per_group, capacity, chosen.shape[1]
        )

        def send(position, inner):
            other = group * per_group + lax.rem(me + position, per_group)

            @pl.when(other != me)
            def _():
                block_copy(other, me, other).start()

            return inner

        lax.fori_loop(0, per_group, send, 0)
        return carry

    lax.fori_loop(0, groups, send_group, 0)
    got_ref[place(me)] = sending[me]

    def finish(step, carry):
        other = lax.rem(me + step, devices)
        copy = block_copy(other, other, other)
        copy.wait_send()
        copy.wait_recv()
        return carry

    lax.fori_loop(1, devices, finish, 0)

    @pl.when(time < times - 1)
    def _():
        halo_copy(time + 1).wait_send()

    fetch_order.wait()
    for station in range(stations):
        total = jnp.zeros((chans * capacity, rows_all), jnp.float32)
        for block in range(times):
            total = total + jnp.dot(
                got_ref[block * chans : (block + 1) * chans].reshape(chans * capacity, rows_all),
                order_ref[block * rows_all : (block + 1) * rows_all, station * rows_all : (station + 1) * rows_all],
                preferred_element_type=jnp.float32,
            )
        out_ref[:, station] = total.astype(jnp.bfloat16).reshape(chans, capacity, rows_all)


def turn(fresh, filter_taps, flagged, owners, table, order, chans, times, capacity):
    devices = chans * times
    pairs, width, channels = fresh.shape
    series = width // 2
    rows = pairs * width
    back = filter_taps.shape[0] // 2
    return pl.pallas_call(
        functools.partial(turn_kernel, chans, times),
        out_shape=jax.ShapeDtypeStruct((chans, series // 2, capacity, rows), jnp.bfloat16),
        in_specs=[pl.BlockSpec(memory_space=pltpu.VMEM)] * 4 + [pl.BlockSpec(memory_space=pl.ANY)] * 2,
        out_specs=pl.BlockSpec(memory_space=pltpu.VMEM),
        scratch_shapes=[
            pltpu.VMEM(table.shape, jnp.bfloat16),
            pltpu.VMEM(order.shape, jnp.bfloat16),
            pltpu.VMEM((back, width, channels), jnp.bfloat16),
            pltpu.VMEM((2 * (back + pairs), series, channels), jnp.float32),
            pltpu.VMEM((rows, 2 * channels), jnp.bfloat16),
            pltpu.VMEM((channels, rows), jnp.bfloat16),
            pltpu.VMEM((devices, capacity, rows), jnp.bfloat16),
            pltpu.VMEM((devices, capacity, rows), jnp.bfloat16),
            pltpu.SemaphoreType.DMA((2,)),
            pltpu.SemaphoreType.DMA((2,)),
            pltpu.SemaphoreType.DMA((devices,)),
            pltpu.SemaphoreType.DMA((devices,)),
        ],
        compiler_params=pltpu.CompilerParams(
            collective_id=0, has_side_effects=True, vmem_limit_bytes=52 * 1024 * 1024
        ),
    )(fresh, filter_taps, flagged.reshape(1, -1), owners.reshape(1, -1), table, order)


def lane_order(stations, spec_dev, blocks):
    shape = (blocks, spec_dev, 2, stations)
    places = np.arange(math.prod(shape)).reshape(shape).transpose(3, 2, 0, 1).reshape(-1)
    table = np.zeros((places.size, places.size), np.float32)
    table[places, np.arange(places.size)] = 1.0
    return jnp.asarray(table.astype(jnp.bfloat16))


def local(voltages, filter_taps, flagged, owners):
    stations, spec_dev, _, channels = voltages.shape
    halo = filter_taps.shape[0] - 1
    chans, times = lax.axis_size("chan"), lax.axis_size("tm")
    devices = chans * times
    capacity = channels // devices
    spectra_all = spec_dev * times
    rows = 2 * stations * spec_dev
    fresh = voltages.transpose(1, 2, 0, 3)
    table = dft_table(channels)
    order = lane_order(stations, spec_dev, times)
    even = halo % 2 == 1 and spec_dev % 2 == 0 and stations % 4 == 0
    if even and capacity % 16 == 0 and GROUP_ROWS % capacity == 0 and channels % GROUP_ROWS == 0:
        paired = fresh.reshape(spec_dev // 2, 4 * stations, channels)
        first = turn(paired, filter_taps, flagged, owners, table, order, chans, times, capacity)
        first = first.reshape(chans * stations, capacity, 2 * spectra_all).transpose(1, 0, 2)
    else:
        fresh = fresh.reshape(spec_dev, 2 * stations, channels)
        before = lax.ppermute(fresh[spec_dev - halo :], "tm", [(i, i + 1) for i in range(times - 1)])
        picks = slot_matrix(flagged, owners, channels, capacity)
        joined = jnp.concatenate([before, fresh]).astype(jnp.float32)
        running = jnp.zeros(fresh.shape, jnp.float32)
        for tap in range(halo + 1):
            start = halo - tap
            running = running + filter_taps[tap] * joined[start : start + spec_dev]
        turned = jnp.concatenate([running[:, stations:], -running[:, :stations]], axis=1)
        both = jnp.concatenate([running, turned], axis=-1).astype(jnp.bfloat16).reshape(rows, 2 * channels)
        spectra = lax.dot_general(
            table, both, (((1,), (1,)), ((), ())), preferred_element_type=jnp.float32
        ).astype(jnp.bfloat16)
        chosen = jnp.dot(picks, spectra, preferred_element_type=jnp.float32).astype(jnp.bfloat16)
        sending = chosen.reshape(devices, capacity, rows)
        received = lax.all_to_all(sending, ("chan", "tm"), split_axis=0, concat_axis=0, tiled=True)
        parts = received.reshape(chans, times, capacity, rows).transpose(0, 2, 1, 3)
        ordered = jnp.dot(
            parts.reshape(chans * capacity, times * rows), order, preferred_element_type=jnp.float32
        ).astype(jnp.bfloat16)
        first = ordered.reshape(chans, capacity, stations, 2 * spectra_all).transpose(1, 0, 2, 3)
        first = first.reshape(capacity, chans * stations, 2 * spectra_all)
    second = jnp.concatenate([first[..., spectra_all:], -first[..., :spectra_all]], axis=-1)
    stacked = jnp.stack([first, second], axis=1)
    total = jnp.einsum("cpit,cjt->cpij", stacked, first, preferred_element_type=jnp.float32)
    return total / spectra_all


def solution(mesh):
    return jax.shard_map(
        local,
        mesh=mesh,
        in_specs=(P("chan", "tm", None, None), P(), P(), P()),
        out_specs=P(("chan", "tm"), None, None, None),
        check_vma=False,
    )
```
